32 devices in a mesh: row: 4 (over z), col: 8 (over y, x, core).
Axes of the slice: x: 2, y: 2, z: 4, core: 2. Of those that a mesh axis runs over, the one named last changes fastest.
Arguments:
- graph_emb: float32 [4096, 256], P('row', 'col'), may hold values from -40 to 40
- conf_emb: float32 [4096, 256], P('col', 'row'), may hold values from -40 to 40
Outputs:
- grad_graph: float32 [4096, 256], P('row', 'col')
- grad_conf: float32 [4096, 256], P('col', 'row')
- row_potential: float32 [4096], P('row')
- col_potential: float32 [4096], P('col')
The draws below stay inside these ranges and needn't reach their ends.
All inputs are finite; a program needn't handle non-finite values.
Results may differ from the reference program's by a relative error of at most 0.0003.
Values sent between devices are 32-bit elements; how exact they have to be, the bound alone decides.
A program may use at most 64 MiB of HBM per device.

```python
import math
import jax
import jax.numpy as jnp
from jax import lax

EMBED = 256
ROWS_DEV = 1024
ITERS = 3
BATCH = 4096


def joint_pair(key):
    base = jax.random.normal(jax.random.fold_in(key, 11), (BATCH, EMBED), jnp.float32)
    row_scale = jnp.exp(jax.random.uniform(jax.random.fold_in(key, 12), (BATCH, 1), jnp.float32, -0.5, 0.5))
    noise = jax.random.normal(jax.random.fold_in(key, 13), (BATCH, EMBED), jnp.float32)
    common = jnp.where(jax.random.uniform(jax.random.fold_in(key, 19), (EMBED,), jnp.float32) < 0.5, -1.0, 1.0).astype(jnp.float32)
    graph_view = base * row_scale + common[None, :]
    conf_view = 0.6 * graph_view + 0.8 * noise
    pair_signs = jnp.where(jax.random.uniform(jax.random.fold_in(key, 15), (BATCH, EMBED // 2), jnp.float32) < 0.5, -1.0, 1.0).astype(jnp.float32)
    alternate = jnp.stack([pair_signs, -pair_signs], axis=2).reshape(BATCH, EMBED)
    level = jax.random.randint(jax.random.fold_in(key, 16), (BATCH, 1), 0, 4).astype(jnp.float32)
    strength = 120.0 + 60.0 * level
    amplitude = jnp.sqrt(strength * EMBED ** (-0.5))
    aligned = amplitude * alternate * common[None, :] + common[None, :]
    index = jnp.arange(BATCH)[:, None]
    first = index % 32 == 0
    second = index % 32 == 1
    repelled = index % 512 == 7
    prior_aligned = jnp.roll(aligned, 1, axis=0)
    prior_strength = jnp.roll(strength, 1, axis=0)
    extra = jax.random.normal(jax.random.fold_in(key, 17), (BATCH, EMBED), jnp.float32)
    near_copy = prior_aligned * (1.0 - 2.0 / prior_strength) + 0.3 * extra
    outlier = -24.0 * common[None, :] + 2.0 * noise
    graph_view = jnp.where(first, aligned, graph_view)
    conf_view = jnp.where(first, aligned, jnp.where(second, near_copy, conf_view))
    conf_view = jnp.where(repelled, outlier, conf_view)
    graph_view = jnp.clip(graph_view, -40.0, 40.0)
    conf_view = jnp.clip(conf_view, -40.0, 40.0)
    order = jax.random.permutation(jax.random.fold_in(key, 18), BATCH)
    return (graph_view[order], conf_view[order])


def draw_graph_emb(key, part):
    return joint_pair(key)[0]


def draw_conf_emb(key, part):
    return joint_pair(key)[1]


def setup_inputs(seed: int = 0) -> dict:
    key_list = jax.random.split(jax.random.key(seed), 3)
    graph_emb = draw_graph_emb(jax.random.fold_in(key_list[2], 71), 0)
    conf_emb = draw_conf_emb(jax.random.fold_in(key_list[2], 71), 0)
    return {"graph_emb": graph_emb, "conf_emb": conf_emb}


entropy_weight = 1.0


def cost_block(graph_part, conf_all):
    products = lax.dot_general(graph_part, conf_all, (((1,), (1,)), ((), ())), precision=lax.Precision.HIGHEST, preferred_element_type=jnp.float32)
    return -products * (EMBED ** -0.5)


def reference(graph_emb, conf_emb):
    block_count = BATCH // ROWS_DEV
    graph_blocks = graph_emb.reshape(block_count, ROWS_DEV, EMBED)
    log_weight = -math.log(BATCH)
    row_pot = jnp.zeros((BATCH,), jnp.float32)
    col_pot = jnp.zeros((BATCH,), jnp.float32)
    for sweep_index in range(ITERS):
        def row_pass(graph_part):
            scores = (col_pot[None, :] - cost_block(graph_part, conf_emb)) / entropy_weight
            peak_value = jnp.max(scores, axis=1)
            return peak_value + jnp.log(jnp.sum(jnp.exp(scores - peak_value[:, None]), axis=1))
        row_lse = lax.map(row_pass, graph_blocks).reshape(BATCH)
        row_pot = entropy_weight * (log_weight - row_lse)
        pot_blocks = row_pot.reshape(block_count, ROWS_DEV)

        def col_step(carry, items):
            running_max, running_sum = carry
            graph_part, pot_part = items
            scores = (pot_part[:, None] - cost_block(graph_part, conf_emb)) / entropy_weight
            new_max = jnp.maximum(running_max, jnp.max(scores, axis=0))
            new_sum = running_sum * jnp.exp(running_max - new_max) + jnp.sum(jnp.exp(scores - new_max[None, :]), axis=0)
            return (new_max, new_sum), None

        start_max = jnp.full((BATCH,), -jnp.inf, jnp.float32)
        start_sum = jnp.zeros((BATCH,), jnp.float32)
        (final_max, final_sum), unused = lax.scan(col_step, (start_max, start_sum), (graph_blocks, pot_blocks))
        col_pot = entropy_weight * (log_weight - (final_max + jnp.log(final_sum)))
    factor = -BATCH * (EMBED ** -0.5)
    pot_blocks = row_pot.reshape(block_count, ROWS_DEV)

    def grad_step(conf_total, items):
        graph_part, pot_part = items
        transport = jnp.exp((pot_part[:, None] + col_pot[None, :] - cost_block(graph_part, conf_emb)) / entropy_weight)
        graph_grad = jnp.dot(transport, conf_emb, precision=lax.Precision.HIGHEST, preferred_element_type=jnp.float32)
        conf_part = lax.dot_general(transport, graph_part, (((0,), (0,)), ((), ())), precision=lax.Precision.HIGHEST, preferred_element_type=jnp.float32)
        return conf_total + conf_part, graph_grad

    conf_total, graph_grads = lax.scan(grad_step, jnp.zeros((BATCH, EMBED), jnp.float32), (graph_blocks, pot_blocks))
    grad_graph = graph_grads.reshape(BATCH, EMBED) * factor
    grad_conf = conf_total * factor
    return (grad_graph, grad_conf, row_pot, col_pot)
```

```python
import functools
import math

import jax
import jax.numpy as jnp
from jax import lax
from jax.experimental import pallas as pl
from jax.experimental.pallas import tpu as pltpu
from jax.sharding import PartitionSpec as P

ITERS = 3
LANES = 128
F32 = jnp.float32
BF16 = jnp.bfloat16


def peer_copy(src, dst, send_sem, recv_sem, axis, peer):
    return pltpu.make_async_remote_copy(
        src_ref=src,
        dst_ref=dst,
        send_sem=send_sem,
        recv_sem=recv_sem,
        device_id={axis: peer},
        device_id_type=pl.DeviceIdType.MESH,
    )


def split(x):
    high = x.astype(BF16)
    return high, (x - high.astype(F32)).astype(BF16)


def dot3(a, b, contract):
    dims = (contract, ((), ()))
    a_high, a_low = a
    b_high, b_low = b
    one = functools.partial(lax.dot_general, dimension_numbers=dims, preferred_element_type=F32)
    return one(a_high, b_high) + (one(a_high, b_low) + one(a_low, b_high))


def over_lanes(row, width):
    return jnp.broadcast_to(row, (width, row.shape[1])).T


def lse_of_rows(score_ref, shift_ref, step):
    rows, width = score_ref.shape
    strips = width // LANES

    def body(index, carry):
        out = []
        at = pl.ds(pl.multiple_of(index * step, step), step)
        shift = shift_ref[at, :]
        for strip in range(strips):
            peak, total = carry[strip]
            x = score_ref[at, strip * LANES:(strip + 1) * LANES] + shift
            x = x.reshape(step // 8, 8, LANES)
            new_peak = jnp.maximum(peak, jnp.max(x, axis=0))
            total = total * jnp.exp(peak - new_peak) + jnp.sum(jnp.exp(x - new_peak[None]), axis=0)
            out.append((new_peak, total))
        return tuple(out)

    start = tuple(
        (jnp.full((8, LANES), -jnp.finfo(F32).max, F32), jnp.zeros((8, LANES), F32))
        for strip in range(strips)
    )
    parts = []
    for peak, total in lax.fori_loop(0, rows // step, body, start):
        top = jnp.max(peak, axis=0, keepdims=True)
        parts.append(top + jnp.log(jnp.sum(total * jnp.exp(peak - top), axis=0, keepdims=True)))
    return jnp.concatenate(parts, axis=1)


def kernel(
    n_row, n_col, f_graph, f_conf,
    graph_ref, conf_ref,
    grad_graph_ref, grad_conf_ref, row_ref, col_ref,
    graph_all, conf_all, score, score_t, row_bcast, col_bcast,
    row_lse, col_lse, graph_part, conf_part, graph_in, conf_in,
    gg_send, gg_recv, gc_send, gc_recv, rl_send, rl_recv, cl_send, cl_recv,
    sg_send, sg_recv, sc_send, sc_recv,
):
    my_row, my_col = lax.axis_index("row"), lax.axis_index("col")
    rows, cols = graph_all.shape[2], conf_all.shape[2]
    embed = n_col * f_graph
    scale = embed ** (-0.5)
    log_weight = -math.log(rows * n_row)

    def col_peer(d):
        return lax.rem(my_col + d, n_col)

    def row_peer(d):
        return lax.rem(my_row + d, n_row)

    def each(count, fn):
        for d in range(1, count):
            fn(d)

    barrier = pltpu.get_barrier_semaphore()

    def greet(axis, peer):
        pl.semaphore_signal(barrier, inc=1, device_id={axis: peer}, device_id_type=pl.DeviceIdType.MESH)

    each(n_col, lambda d: greet("col", col_peer(d)))
    each(n_row, lambda d: greet("row", row_peer(d)))
    graph_all[my_col] = graph_ref[...]
    conf_all[my_row] = conf_ref[...]
    pl.semaphore_wait(barrier, n_col + n_row - 2)

    def gather(axis, peer, buffer, me, slot, send, recv):
        return peer_copy(buffer.at[me], buffer.at[slot], send, recv, axis, peer)

    def graph_copy(d, slot, source):
        return peer_copy(graph_ref, graph_all.at[slot], gg_send.at[d], gg_recv.at[source], "col", col_peer(d))

    def conf_copy(d, slot, source):
        return peer_copy(conf_ref, conf_all.at[slot], gc_send.at[d], gc_recv.at[source], "row", row_peer(d))

    each(n_row, lambda d: conf_copy(d, my_row, my_row).start())
    each(n_col, lambda d: graph_copy(d, my_col, my_col).start())
    each(n_row, lambda d: conf_copy(d, row_peer(d), row_peer(d)).wait_recv())
    each(n_col, lambda d: graph_copy(d, col_peer(d), col_peer(d)).wait_recv())

    def features(buffer, f):
        if buffer.shape[1] == f:
            return buffer[...].reshape(buffer.shape[0] * f, buffer.shape[2])
        return jnp.concatenate([buffer[k][:f] for k in range(buffer.shape[0])], axis=0)

    graph_t = features(graph_all, f_graph)
    conf_t = features(conf_all, f_conf)
    score_t[...] = lax.dot_general(
        conf_t.T, graph_t, (((1,), (0,)), ((), ())),
        precision=lax.Precision.HIGHEST, preferred_element_type=F32,
    ) * scale
    score[...] = score_t[...].T

    col_bcast[...] = jnp.zeros(col_bcast.shape, F32)

    def combine(buffer, it, count):
        parts = [buffer[it, k] for k in range(count)]
        top = functools.reduce(jnp.maximum, parts)
        total = functools.reduce(jnp.add, [jnp.exp(part - top) for part in parts])
        return log_weight - (top + jnp.log(total))

    def row_copy(it, d, slot, source):
        return peer_copy(row_lse.at[it, my_col], row_lse.at[it, slot], rl_send.at[it, d], rl_recv.at[it, source], "col", col_peer(d))

    def col_copy(it, d, slot, source):
        return peer_copy(col_lse.at[it, my_row], col_lse.at[it, slot], cl_send.at[it, d], cl_recv.at[it, source], "row", row_peer(d))

    for it in range(ITERS):
        row_lse[it, my_col] = lse_of_rows(score_t, col_bcast, 64)
        each(n_col, lambda d: row_copy(it, d, my_col, my_col).start())
        each(n_col, lambda d: row_copy(it, d, col_peer(d), col_peer(d)).wait_recv())
        row_pot = combine(row_lse, it, n_col)
        row_bcast[...] = over_lanes(row_pot, LANES)
        col_lse[it, my_row] = lse_of_rows(score, row_bcast, 64)
        each(n_row, lambda d: col_copy(it, d, my_row, my_row).start())
        each(n_row, lambda d: col_copy(it, d, row_peer(d), row_peer(d)).wait_recv())
        col_pot = combine(col_lse, it, n_row)
        if it < ITERS - 1:
            col_bcast[...] = over_lanes(col_pot, LANES)
    row_ref[...] = row_pot
    col_ref[...] = col_pot

    factor = -(rows * n_row) * scale
    plan = jnp.concatenate(
        [
            jnp.exp(score[:, at:at + LANES] + row_bcast[...] + col_pot[:, at:at + LANES])
            for at in range(0, cols, LANES)
        ],
        axis=1,
    )
    plan = split(plan)

    def store(part, block, f):
        if part.shape[1] == f:
            part[...] = block.reshape(part.shape)
        else:
            for k in range(part.shape[0]):
                part[k, 0:f] = block[k * f:(k + 1) * f]
                part[k, f:] = jnp.zeros((part.shape[1] - f, part.shape[2]), F32)

    def conf_scatter(d, block, source):
        return peer_copy(conf_part.at[block], conf_in.at[source], sc_send.at[d], sc_recv.at[source], "row", row_peer(d))

    def graph_scatter(d, block, source):
        return peer_copy(graph_part.at[block], graph_in.at[source], sg_send.at[d], sg_recv.at[source], "col", col_peer(d))

    store(conf_part, dot3(split(graph_t), plan, ((1,), (0,))) * factor, f_conf)
    each(n_row, lambda d: conf_scatter(d, row_peer(d), my_row).start())
    store(graph_part, dot3(split(conf_t), plan, ((1,), (1,))) * factor, f_graph)
    each(n_col, lambda d: graph_scatter(d, col_peer(d), my_col).start())

    each(n_row, lambda d: conf_scatter(d, row_peer(d), row_peer(d)).wait_recv())
    conf_total = conf_part[my_row]
    for d in range(1, n_row):
        conf_total = conf_total + conf_in[row_peer(d)]
    grad_conf_ref[...] = conf_total[:f_conf]
    each(n_col, lambda d: graph_scatter(d, col_peer(d), col_peer(d)).wait_recv())
    graph_total = graph_part[my_col]
    for d in range(1, n_col):
        graph_total = graph_total + graph_in[col_peer(d)]
    grad_graph_ref[...] = graph_total[:f_graph]

    each(n_col, lambda d: graph_copy(d, my_col, my_col).wait_send())
    each(n_row, lambda d: conf_copy(d, my_row, my_row).wait_send())
    for it in range(ITERS):
        each(n_col, lambda d: row_copy(it, d, my_col, my_col).wait_send())
        each(n_row, lambda d: col_copy(it, d, my_row, my_row).wait_send())
    each(n_row, lambda d: conf_scatter(d, row_peer(d), my_row).wait_send())
    each(n_col, lambda d: graph_scatter(d, col_peer(d), my_col).wait_send())


def per_device(n_row, n_col, graph_emb, conf_emb):
    rows, f_graph = graph_emb.shape
    cols, f_conf = conf_emb.shape
    pad_graph, pad_conf = -(-f_graph // 8) * 8, -(-f_conf // 8) * 8
    graph_t = jnp.pad(graph_emb.T, ((0, pad_graph - f_graph), (0, 0)))
    conf_t = jnp.pad(conf_emb.T, ((0, pad_conf - f_conf), (0, 0)))
    vmem = pl.BlockSpec(memory_space=pltpu.VMEM)
    dma = pltpu.SemaphoreType.DMA
    embed = f_graph * n_col
    grad_graph, grad_conf, row_pot, col_pot = pl.pallas_call(
        functools.partial(kernel, n_row, n_col, f_graph, f_conf),
        out_shape=(
            jax.ShapeDtypeStruct((f_graph, rows), F32),
            jax.ShapeDtypeStruct((f_conf, cols), F32),
            jax.ShapeDtypeStruct((1, rows), F32),
            jax.ShapeDtypeStruct((1, cols), F32),
        ),
        in_specs=[vmem] * 2,
        out_specs=[vmem] * 4,
        scratch_shapes=[
            pltpu.VMEM((n_col, pad_graph, rows), F32),
            pltpu.VMEM((n_row, pad_conf, cols), F32),
            pltpu.VMEM((rows, cols), F32),
            pltpu.VMEM((cols, rows), F32),
            pltpu.VMEM((rows, LANES), F32),
            pltpu.VMEM((cols, LANES), F32),
            pltpu.VMEM((ITERS, n_col, 1, rows), F32),
            pltpu.VMEM((ITERS, n_row, 1, cols), F32),
            pltpu.VMEM((n_col, pad_graph, rows), F32),
            pltpu.VMEM((n_row, pad_conf, cols), F32),
            pltpu.VMEM((n_col, pad_graph, rows), F32),
            pltpu.VMEM((n_row, pad_conf, cols), F32),
            dma((n_col,)), dma((n_col,)), dma((n_row,)), dma((n_row,)),
            dma((ITERS, n_col)), dma((ITERS, n_col)), dma((ITERS, n_row)), dma((ITERS, n_row)),
            dma((n_col,)), dma((n_col,)), dma((n_row,)), dma((n_row,)),
        ],
        compiler_params=pltpu.CompilerParams(
            collective_id=0, has_side_effects=True, vmem_limit_bytes=48 * 1024 * 1024
        ),
        cost_estimate=pl.CostEstimate(
            flops=6 * rows * cols * embed, bytes_accessed=16 * rows * embed, transcendentals=7 * rows * cols
        ),
    )(graph_t, conf_t)
    return grad_graph.T, grad_conf.T, row_pot.reshape(rows), col_pot.reshape(cols)


def solution(mesh):
    sizes = dict(mesh.shape)
    return jax.shard_map(
        functools.partial(per_device, sizes["row"], sizes["col"]),
        mesh=mesh,
        in_specs=(P("row", "col"), P("col", "row")),
        out_specs=(P("row", "col"), P("col", "row"), P("row"), P("col")),
        check_vma=False,
    )
```

```python
import functools
import math

import jax
import jax.numpy as jnp
from jax import lax
from jax.experimental import pallas as pl
from jax.experimental.pallas import tpu as pltpu
from jax.sharding import PartitionSpec as P

ITERS = 3
LANES = 128
F32 = jnp.float32
BF16 = jnp.bfloat16


def peer_copy(src, dst, send_sem, recv_sem, axis, peer):
    return pltpu.make_async_remote_copy(
        src_ref=src,
        dst_ref=dst,
        send_sem=send_sem,
        recv_sem=recv_sem,
        device_id={axis: peer},
        device_id_type=pl.DeviceIdType.MESH,
    )


def split(x):
    high = x.astype(BF16)
    return high, (x - high.astype(F32)).astype(BF16)


def dot3(a, b, contract):
    dims = (contract, ((), ()))
    a_high, a_low = a
    b_high, b_low = b
    one = functools.partial(lax.dot_general, dimension_numbers=dims, preferred_element_type=F32)
    return one(a_high, b_high) + (one(a_high, b_low) + one(a_low, b_high))


def flip(me, d):
    out = me
    bit = 1
    while bit <= d:
        if d & bit:
            out = out + bit * (1 - 2 * lax.rem(me // bit, 2))
        bit *= 2
    return out


def over_lanes(row, width):
    return jnp.broadcast_to(row, (width, row.shape[1])).T


def lse_of_rows(score_ref, shift_ref, step):
    rows, width = score_ref.shape
    strips = width // LANES

    def body(index, carry):
        out = []
        at = pl.ds(pl.multiple_of(index * step, step), step)
        shift = shift_ref[at, :]
        for strip in range(strips):
            peak, total = carry[strip]
            x = score_ref[at, strip * LANES:(strip + 1) * LANES] + shift
            x = x.reshape(step // 8, 8, LANES)
            new_peak = jnp.maximum(peak, jnp.max(x, axis=0))
            total = total * jnp.exp(peak - new_peak) + jnp.sum(jnp.exp(x - new_peak[None]), axis=0)
            out.append((new_peak, total))
        return tuple(out)

    start = tuple(
        (jnp.full((8, LANES), -jnp.finfo(F32).max, F32), jnp.zeros((8, LANES), F32))
        for strip in range(strips)
    )
    parts = []
    for peak, total in lax.fori_loop(0, rows // step, body, start):
        top = jnp.max(peak, axis=0, keepdims=True)
        parts.append(top + jnp.log(jnp.sum(total * jnp.exp(peak - top), axis=0, keepdims=True)))
    return jnp.concatenate(parts, axis=1)


def kernel(
    n_row, n_col, f_graph, f_conf,
    graph_ref, conf_ref,
    grad_graph_ref, grad_conf_ref, row_ref, col_ref,
    graph_all, conf_all, score, score_t, row_bcast, col_bcast,
    row_lse, col_lse, graph_part, conf_part, graph_in, conf_in,
    gg_send, gg_recv, gc_send, gc_recv, rl_send, rl_recv, cl_send, cl_recv,
    sg_send, sg_recv, sc_send, sc_recv, pre_recv, graph_pre, conf_pre,
):
    my_row, my_col = lax.axis_index("row"), lax.axis_index("col")
    rows, cols = graph_all.shape[2], conf_all.shape[2]
    embed = n_col * f_graph
    scale = embed ** (-0.5)
    log_weight = -math.log(rows * n_row)

    def col_peer(d):
        return flip(my_col, d)

    def row_peer(d):
        return flip(my_row, d)

    def each(count, fn):
        for d in range(1, count):
            fn(d)

    layered = (n_row, n_col) == (4, 8)
    inner = (my_row + 1) // 2 == 1
    barrier = pltpu.get_barrier_semaphore()

    def greet(axis, peer):
        pl.semaphore_signal(barrier, inc=1, device_id={axis: peer}, device_id_type=pl.DeviceIdType.MESH)

    each(n_col, lambda d: greet("col", col_peer(d)))
    each(n_row, lambda d: greet("row", row_peer(d)))
    graph_own = pltpu.make_async_copy(graph_ref, graph_all.at[my_col], gg_recv.at[my_col])
    conf_own = pltpu.make_async_copy(conf_ref, conf_all.at[my_row], gc_recv.at[my_row])
    graph_own.start()
    conf_own.start()
    pl.semaphore_wait(barrier, n_col + n_row - 2)

    def graph_copy(d):
        return peer_copy(graph_ref, graph_all.at[my_col], gg_send.at[d], gg_recv.at[my_col], "col", col_peer(d))

    def graph_pass(d):
        slot = graph_all.at[col_peer(d)]
        return peer_copy(slot, slot, gg_send.at[d + 1], gg_recv.at[col_peer(d)], "col", col_peer(1))

    def graph_wait(d):
        slot = graph_all.at[col_peer(d)]
        peer_copy(slot, slot, gg_send.at[d], gg_recv.at[col_peer(d)], "col", col_peer(d)).wait_recv()

    def conf_copy(d):
        return peer_copy(conf_ref, conf_all.at[my_row], gc_send.at[d], gc_recv.at[my_row], "row", row_peer(d))

    def conf_pass():
        slot = conf_all.at[row_peer(2)]
        return peer_copy(slot, slot, gc_send.at[0], gc_recv.at[row_peer(2)], "row", row_peer(1))

    def conf_wait(d):
        slot = conf_all.at[row_peer(d)]
        peer_copy(slot, slot, gc_send.at[d], gc_recv.at[row_peer(d)], "row", row_peer(d)).wait_recv()

    if layered:
        conf_copy(2).start()
        for d in (6, 2, 4, 1):
            graph_copy(d).start()
        conf_copy(1).start()
        pl.when(inner)(lambda: conf_copy(3).start())
        for d in (2, 4):
            graph_wait(d)
            graph_pass(d).start()
        conf_wait(2)
        pl.when(inner)(lambda: conf_pass().start())
        graph_wait(6)
        graph_pass(6).start()
        conf_wait(1)
        conf_wait(3)
        for d in (1, 3, 5, 7):
            graph_wait(d)
    else:
        each(n_row, lambda d: conf_copy(d).start())
        each(n_col, lambda d: graph_copy(d).start())
        each(n_row, conf_wait)
        each(n_col, graph_wait)
    graph_own.wait()
    conf_own.wait()

    def features(buffer, f):
        if buffer.shape[1] == f:
            return buffer[...].reshape(buffer.shape[0] * f, buffer.shape[2])
        return jnp.concatenate([buffer[k][:f] for k in range(buffer.shape[0])], axis=0)

    graph_t = features(graph_all, f_graph)
    conf_t = features(conf_all, f_conf)
    score_t[...] = lax.dot_general(
        conf_t.T, graph_t, (((1,), (0,)), ((), ())),
        precision=lax.Precision.HIGHEST, preferred_element_type=F32,
    ) * scale
    score[...] = score_t[...].T

    col_bcast[...] = jnp.zeros(col_bcast.shape, F32)

    def combine(buffer, it, count):
        parts = [buffer[it, k] for k in range(count)]
        top = functools.reduce(jnp.maximum, parts)
        total = functools.reduce(jnp.add, [jnp.exp(part - top) for part in parts])
        return log_weight - (top + jnp.log(total))

    def row_copy(it, d, slot, source):
        return peer_copy(row_lse.at[it, my_col], row_lse.at[it, slot], rl_send.at[it, d], rl_recv.at[it, source], "col", col_peer(d))

    def col_copy(it, d, slot, source):
        return peer_copy(col_lse.at[it, my_row], col_lse.at[it, slot], cl_send.at[it, d], cl_recv.at[it, source], "row", row_peer(d))

    for it in range(ITERS):
        row_lse[it, my_col] = lse_of_rows(score_t, col_bcast, 64)
        each(n_col, lambda d: row_copy(it, d, my_col, my_col).start())
        each(n_col, lambda d: row_copy(it, d, col_peer(d), col_peer(d)).wait_recv())
        row_pot = combine(row_lse, it, n_col)
        row_bcast[...] = over_lanes(row_pot, LANES)
        col_lse[it, my_row] = lse_of_rows(score, row_bcast, 64)
        each(n_row, lambda d: col_copy(it, d, my_row, my_row).start())
        each(n_row, lambda d: col_copy(it, d, row_peer(d), row_peer(d)).wait_recv())
        col_pot = combine(col_lse, it, n_row)
        if it < ITERS - 1:
            col_bcast[...] = over_lanes(col_pot, LANES)
    row_ref[...] = row_pot
    col_ref[...] = col_pot

    factor = -(rows * n_row) * scale
    plan = jnp.concatenate(
        [
            jnp.exp(score[:, at:at + LANES] + row_bcast[...] + col_pot[:, at:at + LANES])
            for at in range(0, cols, LANES)
        ],
        axis=1,
    )
    plan = split(plan)

    def store(part, block, f):
        if part.shape[1] == f:
            part[...] = block.reshape(part.shape)
        else:
            for k in range(part.shape[0]):
                part[k, 0:f] = block[k * f:(k + 1) * f]
                part[k, f:] = jnp.zeros((part.shape[1] - f, part.shape[2]), F32)

    def conf_scatter(d):
        return peer_copy(
            conf_part.at[row_peer(d)], conf_in.at[my_row], sc_send.at[d], sc_recv.at[my_row], "row", row_peer(d)
        )

    def conf_arrive(d):
        slot = conf_in.at[row_peer(d)]
        peer_copy(slot, slot, sc_send.at[d], sc_recv.at[row_peer(d)], "row", row_peer(d)).wait_recv()

    def conf_early():
        return peer_copy(
            conf_part.at[row_peer(3)], conf_pre, sc_send.at[3], pre_recv.at[n_col], "row", row_peer(1)
        )

    def graph_scatter(d):
        return peer_copy(
            graph_part.at[col_peer(d)], graph_in.at[my_col], sg_send.at[d], sg_recv.at[my_col], "col", col_peer(d)
        )

    def graph_arrive(d):
        slot = graph_in.at[col_peer(d)]
        peer_copy(slot, slot, sg_send.at[d], sg_recv.at[col_peer(d)], "col", col_peer(d)).wait_recv()

    def graph_early(d):
        return peer_copy(
            graph_part.at[col_peer(d)], graph_pre.at[d // 2], sg_send.at[d], pre_recv.at[d // 2], "col", col_peer(1)
        )

    store(graph_part, dot3(split(conf_t), plan, ((1,), (1,))) * factor, f_graph)
    if layered:
        for d in (7, 3, 5, 1):
            graph_early(d).start()
    else:
        each(n_col, lambda d: graph_scatter(d).start())
    store(conf_part, dot3(split(graph_t), plan, ((1,), (0,))) * factor, f_conf)
    if layered:

        @pl.when(inner)
        def _():
            conf_scatter(1).start()
            conf_scatter(3).start()

        @pl.when(jnp.logical_not(inner))
        def _():
            conf_early().start()
            conf_scatter(2).start()
            conf_scatter(1).start()

        for d in (6, 2, 4):
            graph_early(d + 1).wait_recv()
            graph_part[col_peer(d)] = graph_part[col_peer(d)] + graph_pre[d // 2]
            graph_scatter(d).start()

        @pl.when(inner)
        def _():
            conf_early().wait_recv()
            conf_part[row_peer(2)] = conf_part[row_peer(2)] + conf_pre[...]
            conf_scatter(2).start()

        graph_early(1).wait_recv()
        graph_total = graph_part[my_col] + graph_pre[0]
        for d in (2, 4, 6):
            graph_arrive(d)
            graph_total = graph_total + graph_in[col_peer(d)]
        grad_graph_ref[...] = graph_total[:f_graph]
        conf_total = conf_part[my_row]
        for d in (1, 2):
            conf_arrive(d)
            conf_total = conf_total + conf_in[row_peer(d)]
        grad_conf_ref[...] = conf_total[:f_conf]

        @pl.when(inner)
        def _():
            conf_arrive(3)
            grad_conf_ref[...] = grad_conf_ref[...] + conf_in[row_peer(3)][:f_conf]

    else:
        each(n_row, lambda d: conf_scatter(d).start())
        each(n_row, conf_arrive)
        conf_total = conf_part[my_row]
        for d in range(1, n_row):
            conf_total = conf_total + conf_in[row_peer(d)]
        grad_conf_ref[...] = conf_total[:f_conf]
        each(n_col, graph_arrive)
        graph_total = graph_part[my_col]
        for d in range(1, n_col):
            graph_total = graph_total + graph_in[col_peer(d)]
        grad_graph_ref[...] = graph_total[:f_graph]

    if layered:
        for d in (1, 2, 4, 6):
            graph_copy(d).wait_send()
        for d in (2, 4, 6):
            graph_pass(d).wait_send()
            graph_scatter(d).wait_send()
        for d in (1, 3, 5, 7):
            graph_early(d).wait_send()
        for d in (1, 2):
            conf_copy(d).wait_send()
            conf_scatter(d).wait_send()

        @pl.when(inner)
        def _():
            conf_copy(3).wait_send()
            conf_pass().wait_send()
            conf_scatter(3).wait_send()

        @pl.when(jnp.logical_not(inner))
        def _():
            conf_early().wait_send()

    else:
        each(n_col, lambda d: graph_copy(d).wait_send())
        each(n_row, lambda d: conf_copy(d).wait_send())
        each(n_row, lambda d: conf_scatter(d).wait_send())
        each(n_col, lambda d: graph_scatter(d).wait_send())
    for it in range(ITERS):
        each(n_col, lambda d: row_copy(it, d, my_col, my_col).wait_send())
        each(n_row, lambda d: col_copy(it, d, my_row, my_row).wait_send())


def flush(*refs):
    count = len(refs) // 2
    sems = refs[-1]
    copies = [pltpu.make_async_copy(refs[k], refs[count + k], sems.at[k]) for k in range(count)]
    for copy in copies:
        copy.start()
    for copy in copies:
        copy.wait()


def per_device(n_row, n_col, graph_emb, conf_emb):
    rows, f_graph = graph_emb.shape
    cols, f_conf = conf_emb.shape
    pad_graph, pad_conf = -(-f_graph // 8) * 8, -(-f_conf // 8) * 8
    graph_t = jnp.pad(graph_emb.T, ((0, pad_graph - f_graph), (0, 0)))
    conf_t = jnp.pad(conf_emb.T, ((0, pad_conf - f_conf), (0, 0)))
    vmem = pl.BlockSpec(memory_space=pltpu.VMEM)
    hbm = pl.BlockSpec(memory_space=pltpu.HBM)
    dma = pltpu.SemaphoreType.DMA
    embed = f_graph * n_col
    parts = pl.pallas_call(
        functools.partial(kernel, n_row, n_col, f_graph, f_conf),
        out_shape=(
            jax.ShapeDtypeStruct((f_graph, rows), F32),
            jax.ShapeDtypeStruct((f_conf, cols), F32),
            jax.ShapeDtypeStruct((1, rows), F32),
            jax.ShapeDtypeStruct((1, cols), F32),
        ),
        in_specs=[hbm] * 2,
        out_specs=[vmem] * 4,
        scratch_shapes=[
            pltpu.VMEM((n_col, pad_graph, rows), F32),
            pltpu.VMEM((n_row, pad_conf, cols), F32),
            pltpu.VMEM((rows, cols), F32),
            pltpu.VMEM((cols, rows), F32),
            pltpu.VMEM((rows, LANES), F32),
            pltpu.VMEM((cols, LANES), F32),
            pltpu.VMEM((ITERS, n_col, 1, rows), F32),
            pltpu.VMEM((ITERS, n_row, 1, cols), F32),
            pltpu.VMEM((n_col, pad_graph, rows), F32),
            pltpu.VMEM((n_row, pad_conf, cols), F32),
            pltpu.VMEM((n_col, pad_graph, rows), F32),
            pltpu.VMEM((n_row, pad_conf, cols), F32),
            dma((n_col,)), dma((n_col,)), dma((n_row,)), dma((n_row,)),
            dma((ITERS, n_col)), dma((ITERS, n_col)), dma((ITERS, n_row)), dma((ITERS, n_row)),
            dma((n_col,)), dma((n_col,)), dma((n_row,)), dma((n_row,)), dma((n_col + 1,)),
            pltpu.VMEM((max(n_col // 2, 1), pad_graph, rows), F32),
            pltpu.VMEM((pad_conf, cols), F32),
        ],
        compiler_params=pltpu.CompilerParams(
            collective_id=0, has_side_effects=True, vmem_limit_bytes=60 * 1024 * 1024
        ),
        cost_estimate=pl.CostEstimate(
            flops=6 * rows * cols * embed, bytes_accessed=16 * rows * embed, transcendentals=7 * rows * cols
        ),
    )(graph_t, conf_t)
    grad_graph, grad_conf, row_pot, col_pot = pl.pallas_call(
        flush,
        out_shape=tuple(jax.ShapeDtypeStruct(part.shape, F32) for part in parts),
        in_specs=[pl.BlockSpec(memory_space=pl.ANY)] * 4,
        out_specs=[hbm] * 4,
        scratch_shapes=[dma((4,))],
    )(*parts)
    return grad_graph.T, grad_conf.T, row_pot.reshape(rows), col_pot.reshape(cols)


def solution(mesh):
    sizes = dict(mesh.shape)
    return jax.shard_map(
        functools.partial(per_device, sizes["row"], sizes["col"]),
        mesh=mesh,
        in_specs=(P("row", "col"), P("col", "row")),
        out_specs=(P("row", "col"), P("col", "row"), P("row"), P("col")),
        check_vma=False,
    )
```

```python
import functools
import math

import jax
import jax.numpy as jnp
from jax import lax
from jax.experimental import pallas as pl
from jax.experimental.pallas import tpu as pltpu
from jax.sharding import PartitionSpec as P

ITERS = 3
LANES = 128
F32 = jnp.float32
BF16 = jnp.bfloat16


def peer_copy(src, dst, send_sem, recv_sem, axis, peer):
    return pltpu.make_async_remote_copy(
        src_ref=src,
        dst_ref=dst,
        send_sem=send_sem,
        recv_sem=recv_sem,
        device_id={axis: peer},
        device_id_type=pl.DeviceIdType.MESH,
    )


def split(x):
    high = x.astype(BF16)
    return high, (x - high.astype(F32)).astype(BF16)


def dot3(a, b, contract):
    dims = (contract, ((), ()))
    a_high, a_low = a
    b_high, b_low = b
    one = functools.partial(lax.dot_general, dimension_numbers=dims, preferred_element_type=F32)
    return one(a_high, b_high) + (one(a_high, b_low) + one(a_low, b_high))


def flip(me, d):
    out = me
    bit = 1
    while bit <= d:
        if d & bit:
            out = out + bit * (1 - 2 * lax.rem(me // bit, 2))
        bit *= 2
    return out


def over_lanes(row, width):
    return jnp.broadcast_to(row, (width, row.shape[1])).T


def lse_of_rows(score_ref, shift_ref, step):
    rows, width = score_ref.shape
    strips = width // LANES

    def body(index, carry):
        out = []
        at = pl.ds(pl.multiple_of(index * step, step), step)
        shift = shift_ref[at, :]
        for strip in range(strips):
            peak, total = carry[strip]
            x = score_ref[at, strip * LANES:(strip + 1) * LANES] + shift
            x = x.reshape(step // 8, 8, LANES)
            new_peak = jnp.maximum(peak, jnp.max(x, axis=0))
            total = total * jnp.exp(peak - new_peak) + jnp.sum(jnp.exp(x - new_peak[None]), axis=0)
            out.append((new_peak, total))
        return tuple(out)

    start = tuple(
        (jnp.full((8, LANES), -jnp.finfo(F32).max, F32), jnp.zeros((8, LANES), F32))
        for strip in range(strips)
    )
    parts = []
    for peak, total in lax.fori_loop(0, rows // step, body, start):
        top = jnp.max(peak, axis=0, keepdims=True)
        parts.append(top + jnp.log(jnp.sum(total * jnp.exp(peak - top), axis=0, keepdims=True)))
    return jnp.concatenate(parts, axis=1)


def kernel(
    n_row, n_col, f_graph, f_conf,
    graph_ref, conf_ref,
    grad_graph_ref, grad_conf_ref, row_ref, col_ref,
    graph_all, conf_all, score, score_t, row_bcast, col_bcast,
    row_lse, col_lse, graph_part, conf_part, graph_in, conf_in,
    gg_send, gg_recv, gc_send, gc_recv, rl_send, rl_recv, cl_send, cl_recv,
    sg_send, sg_recv, sc_send, sc_recv, pre_recv, graph_pre, conf_pre,
):
    my_row, my_col = lax.axis_index("row"), lax.axis_index("col")
    rows, cols = graph_all.shape[2], conf_all.shape[2]
    embed = n_col * f_graph
    scale = embed ** (-0.5)
    log_weight = -math.log(rows * n_row)

    def col_peer(d):
        return flip(my_col, d)

    def row_peer(d):
        return flip(my_row, d)

    def each(count, fn):
        for d in range(1, count):
            fn(d)

    gz = gxy = sz = sxy = (n_row, n_col) == (4, 8)
    inner = (my_row + 1) // 2 == 1
    barrier = pltpu.get_barrier_semaphore()

    def greet(axis, peer):
        pl.semaphore_signal(barrier, inc=1, device_id={axis: peer}, device_id_type=pl.DeviceIdType.MESH)

    each(n_col, lambda d: greet("col", col_peer(d)))
    each(n_row, lambda d: greet("row", row_peer(d)))
    graph_own = pltpu.make_async_copy(graph_ref, graph_all.at[my_col], gg_recv.at[my_col])
    conf_own = pltpu.make_async_copy(conf_ref, conf_all.at[my_row], gc_recv.at[my_row])
    graph_own.start()
    conf_own.start()
    pl.semaphore_wait(barrier, n_col + n_row - 2)

    def graph_copy(d):
        return peer_copy(graph_ref, graph_all.at[my_col], gg_send.at[d], gg_recv.at[my_col], "col", col_peer(d))

    def graph_pass(d):
        slot = graph_all.at[col_peer(d)]
        return peer_copy(slot, slot, gg_send.at[d + 1], gg_recv.at[col_peer(d)], "col", col_peer(1))

    def graph_wait(d):
        slot = graph_all.at[col_peer(d)]
        peer_copy(slot, slot, gg_send.at[d], gg_recv.at[col_peer(d)], "col", col_peer(d)).wait_recv()

    def conf_copy(d):
        return peer_copy(conf_ref, conf_all.at[my_row], gc_send.at[d], gc_recv.at[my_row], "row", row_peer(d))

    def conf_pass():
        slot = conf_all.at[row_peer(2)]
        return peer_copy(slot, slot, gc_send.at[0], gc_recv.at[row_peer(2)], "row", row_peer(1))

    def conf_wait(d):
        slot = conf_all.at[row_peer(d)]
        peer_copy(slot, slot, gc_send.at[d], gc_recv.at[row_peer(d)], "row", row_peer(d)).wait_recv()

    if gz:
        conf_copy(2).start()
    else:
        each(n_row, lambda d: conf_copy(d).start())
    for d in (6, 2, 4, 1) if gxy else range(1, n_col):
        graph_copy(d).start()
    if gz:
        conf_copy(1).start()
        pl.when(inner)(lambda: conf_copy(3).start())
    if gxy:
        for d in (2, 4):
            graph_wait(d)
            graph_pass(d).start()
    if gz:
        conf_wait(2)
        pl.when(inner)(lambda: conf_pass().start())
    if gxy:
        graph_wait(6)
        graph_pass(6).start()
    for d in (1, 3) if gz else range(1, n_row):
        conf_wait(d)
    for d in (1, 3, 5, 7) if gxy else range(1, n_col):
        graph_wait(d)
    graph_own.wait()
    conf_own.wait()

    def features(buffer, f):
        if buffer.shape[1] == f:
            return buffer[...].reshape(buffer.shape[0] * f, buffer.shape[2])
        return jnp.concatenate([buffer[k][:f] for k in range(buffer.shape[0])], axis=0)

    graph_t = features(graph_all, f_graph)
    conf_t = features(conf_all, f_conf)
    score_t[...] = lax.dot_general(
        conf_t.T, graph_t, (((1,), (0,)), ((), ())),
        precision=lax.Precision.HIGHEST, preferred_element_type=F32,
    ) * scale
    score[...] = score_t[...].T

    col_bcast[...] = jnp.zeros(col_bcast.shape, F32)

    def combine(buffer, it, count):
        parts = [buffer[it, k] for k in range(count)]
        top = functools.reduce(jnp.maximum, parts)
        total = functools.reduce(jnp.add, [jnp.exp(part - top) for part in parts])
        return log_weight - (top + jnp.log(total))

    def row_copy(it, d, slot, source):
        return peer_copy(row_lse.at[it, my_col], row_lse.at[it, slot], rl_send.at[it, d], rl_recv.at[it, source], "col", col_peer(d))

    def col_copy(it, d, slot, source):
        return peer_copy(col_lse.at[it, my_row], col_lse.at[it, slot], cl_send.at[it, d], cl_recv.at[it, source], "row", row_peer(d))

    for it in range(ITERS):
        row_lse[it, my_col] = lse_of_rows(score_t, col_bcast, 64)
        each(n_col, lambda d: row_copy(it, d, my_col, my_col).start())
        each(n_col, lambda d: row_copy(it, d, col_peer(d), col_peer(d)).wait_recv())
        row_pot = combine(row_lse, it, n_col)
        row_bcast[...] = over_lanes(row_pot, LANES)
        col_lse[it, my_row] = lse_of_rows(score, row_bcast, 64)
        each(n_row, lambda d: col_copy(it, d, my_row, my_row).start())
        each(n_row, lambda d: col_copy(it, d, row_peer(d), row_peer(d)).wait_recv())
        col_pot = combine(col_lse, it, n_row)
        if it < ITERS - 1:
            col_bcast[...] = over_lanes(col_pot, LANES)
    row_ref[...] = row_pot
    col_ref[...] = col_pot

    factor = -(rows * n_row) * scale
    plan = jnp.concatenate(
        [
            jnp.exp(score[:, at:at + LANES] + row_bcast[...] + col_pot[:, at:at + LANES])
            for at in range(0, cols, LANES)
        ],
        axis=1,
    )
    plan = split(plan)

    def store(part, block, f):
        if part.shape[1] == f:
            part[...] = block.reshape(part.shape)
        else:
            for k in range(part.shape[0]):
                part[k, 0:f] = block[k * f:(k + 1) * f]
                part[k, f:] = jnp.zeros((part.shape[1] - f, part.shape[2]), F32)

    def conf_scatter(d):
        return peer_copy(
            conf_part.at[row_peer(d)], conf_in.at[my_row], sc_send.at[d], sc_recv.at[my_row], "row", row_peer(d)
        )

    def conf_arrive(d):
        slot = conf_in.at[row_peer(d)]
        peer_copy(slot, slot, sc_send.at[d], sc_recv.at[row_peer(d)], "row", row_peer(d)).wait_recv()

    def conf_early():
        return peer_copy(
            conf_part.at[row_peer(3)], conf_pre, sc_send.at[3], pre_recv.at[n_col], "row", row_peer(1)
        )

    def graph_scatter(d):
        return peer_copy(
            graph_part.at[col_peer(d)], graph_in.at[my_col], sg_send.at[d], sg_recv.at[my_col], "col", col_peer(d)
        )

    def graph_arrive(d):
        slot = graph_in.at[col_peer(d)]
        peer_copy(slot, slot, sg_send.at[d], sg_recv.at[col_peer(d)], "col", col_peer(d)).wait_recv()

    def graph_early(d):
        return peer_copy(
            graph_part.at[col_peer(d)], graph_pre.at[d // 2], sg_send.at[d], pre_recv.at[d // 2], "col", col_peer(1)
        )

    store(graph_part, dot3(split(conf_t), plan, ((1,), (1,))) * factor, f_graph)
    if sxy:
        for d in (7, 3, 5, 1):
            graph_early(d).start()
    else:
        each(n_col, lambda d: graph_scatter(d).start())
    store(conf_part, dot3(split(graph_t), plan, ((1,), (0,))) * factor, f_conf)
    if sz:

        @pl.when(inner)
        def _():
            conf_scatter(1).start()
            conf_scatter(3).start()

        @pl.when(jnp.logical_not(inner))
        def _():
            conf_early().start()
            conf_scatter(2).start()
            conf_scatter(1).start()

    else:
        each(n_row, lambda d: conf_scatter(d).start())

    if sxy:
        for d in (6, 2, 4):
            graph_early(d + 1).wait_recv()
            graph_part[col_peer(d)] = graph_part[col_peer(d)] + graph_pre[d // 2]
            graph_scatter(d).start()

    if sz:

        @pl.when(inner)
        def _():
            conf_early().wait_recv()
            conf_part[row_peer(2)] = conf_part[row_peer(2)] + conf_pre[...]
            conf_scatter(2).start()

    graph_total = graph_part[my_col]
    if sxy:
        graph_early(1).wait_recv()
        graph_total = graph_total + graph_pre[0]
    for d in (2, 4, 6) if sxy else range(1, n_col):
        graph_arrive(d)
        graph_total = graph_total + graph_in[col_peer(d)]
    grad_graph_ref[...] = graph_total[:f_graph]
    conf_total = conf_part[my_row]
    for d in (1, 2) if sz else range(1, n_row):
        conf_arrive(d)
        conf_total = conf_total + conf_in[row_peer(d)]
    grad_conf_ref[...] = conf_total[:f_conf]
    if sz:

        @pl.when(inner)
        def _():
            conf_arrive(3)
            grad_conf_ref[...] = grad_conf_ref[...] + conf_in[row_peer(3)][:f_conf]

    for d in (1, 2, 4, 6) if gxy else range(1, n_col):
        graph_copy(d).wait_send()
    if gxy:
        for d in (2, 4, 6):
            graph_pass(d).wait_send()
    for d in (2, 4, 6) if sxy else range(1, n_col):
        graph_scatter(d).wait_send()
    if sxy:
        for d in (1, 3, 5, 7):
            graph_early(d).wait_send()
    for d in (1, 2) if gz else range(1, n_row):
        conf_copy(d).wait_send()
    for d in (1, 2) if sz else range(1, n_row):
        conf_scatter(d).wait_send()

    @pl.when(inner)
    def _():
        if gz:
            conf_copy(3).wait_send()
            conf_pass().wait_send()
        if sz:
            conf_scatter(3).wait_send()

    if sz:
        pl.when(jnp.logical_not(inner))(lambda: conf_early().wait_send())
    for it in range(ITERS):
        each(n_col, lambda d: row_copy(it, d, my_col, my_col).wait_send())
        each(n_row, lambda d: col_copy(it, d, my_row, my_row).wait_send())


def flush(*refs):
    count = len(refs) // 2
    for k in range(count):
        refs[count + k][...] = refs[k][...]


def per_device(n_row, n_col, graph_emb, conf_emb):
    rows, f_graph = graph_emb.shape
    cols, f_conf = conf_emb.shape
    pad_graph, pad_conf = -(-f_graph // 8) * 8, -(-f_conf // 8) * 8
    graph_t = jnp.pad(graph_emb.T, ((0, pad_graph - f_graph), (0, 0)))
    conf_t = jnp.pad(conf_emb.T, ((0, pad_conf - f_conf), (0, 0)))
    vmem = pl.BlockSpec(memory_space=pltpu.VMEM)
    hbm = pl.BlockSpec(memory_space=pltpu.HBM)
    dma = pltpu.SemaphoreType.DMA
    embed = f_graph * n_col
    parts = pl.pallas_call(
        functools.partial(kernel, n_row, n_col, f_graph, f_conf),
        out_shape=(
            jax.ShapeDtypeStruct((f_graph, rows), F32),
            jax.ShapeDtypeStruct((f_conf, cols), F32),
            jax.ShapeDtypeStruct((1, rows), F32),
            jax.ShapeDtypeStruct((1, cols), F32),
        ),
        in_specs=[hbm] * 2,
        out_specs=[vmem] * 4,
        scratch_shapes=[
            pltpu.VMEM((n_col, pad_graph, rows), F32),
            pltpu.VMEM((n_row, pad_conf, cols), F32),
            pltpu.VMEM((rows, cols), F32),
            pltpu.VMEM((cols, rows), F32),
            pltpu.VMEM((rows, LANES), F32),
            pltpu.VMEM((cols, LANES), F32),
            pltpu.VMEM((ITERS, n_col, 1, rows), F32),
            pltpu.VMEM((ITERS, n_row, 1, cols), F32),
            pltpu.VMEM((n_col, pad_graph, rows), F32),
            pltpu.VMEM((n_row, pad_conf, cols), F32),
            pltpu.VMEM((n_col, pad_graph, rows), F32),
            pltpu.VMEM((n_row, pad_conf, cols), F32),
            dma((n_col,)), dma((n_col,)), dma((n_row,)), dma((n_row,)),
            dma((ITERS, n_col)), dma((ITERS, n_col)), dma((ITERS, n_row)), dma((ITERS, n_row)),
            dma((n_col,)), dma((n_col,)), dma((n_row,)), dma((n_row,)), dma((n_col + 1,)),
            pltpu.VMEM((max(n_col // 2, 1), pad_graph, rows), F32),
            pltpu.VMEM((pad_conf, cols), F32),
        ],
        compiler_params=pltpu.CompilerParams(
            collective_id=0, has_side_effects=True, vmem_limit_bytes=60 * 1024 * 1024
        ),
        cost_estimate=pl.CostEstimate(
            flops=6 * rows * cols * embed, bytes_accessed=16 * rows * embed, transcendentals=7 * rows * cols
        ),
    )(graph_t, conf_t)
    grad_graph, grad_conf, row_pot, col_pot = pl.pallas_call(
        flush,
        out_shape=tuple(jax.ShapeDtypeStruct(part.shape, F32) for part in parts),
        in_specs=[vmem] * 4,
        out_specs=[vmem] * 4,
    )(*parts)
    return grad_graph.T, grad_conf.T, row_pot.reshape(rows), col_pot.reshape(cols)


def solution(mesh):
    sizes = dict(mesh.shape)
    return jax.shard_map(
        functools.partial(per_device, sizes["row"], sizes["col"]),
        mesh=mesh,
        in_specs=(P("row", "col"), P("col", "row")),
        out_specs=(P("row", "col"), P("col", "row"), P("row"), P("col")),
        check_vma=False,
    )
```
